32 devices in a mesh: traj: 16 (over z, x, core), lat: 2 (over y).
Axes of the slice: x: 2, y: 2, z: 4, core: 2. Of those that a mesh axis runs over, the one named last changes fastest.
Arguments:
- ensemble: float32 [16, 56, 192, 384], P('traj', None, 'lat'), may hold values from -4 to 4
- counts: int32 [16], P('traj'), may hold values from 0 to 4, as said below
- mixing: bfloat16 [56, 56], replicated, may hold values from -0.75 to 0.75
- weights: float32 [192], P('lat'), may hold values from 0.5 to 1.5
- legendre: bfloat16 [128, 192, 128], P('lat'), may hold values from -0.5 to 0.5
- to_modes: float32 [56, 56], replicated, may hold values from -0.75 to 0.75
- from_modes: float32 [56, 56], replicated, may hold values from -0.75 to 0.75
- mode_rates: float32 [56], replicated, may hold values from 0.1 to 10
Outputs:
- advanced: float32 [16, 56, 192, 384], P('traj', None, 'lat')
The draws below stay inside these ranges and needn't reach their ends.
Inputs may be any that keep to these rules, and one draw needn't show every extreme that they name: The counts of all members sum to 16, and some member has exactly 4.
All inputs are finite; a program needn't handle non-finite values.
Results may differ from the reference program's by a relative error of at most 0.015.
Values may be sent and summed in bfloat16 or wider, within the bound.
A program may use at most 64 MiB of HBM per device.

```python
import math
import jax
import jax.numpy as jnp
from jax import lax

NLON = 384
NLAT = 192
M = 128
NTOT = 128
LEV = 56
MEMBERS = 16


def draw_counts(key, part):
    key_one, key_two, key_three = jax.random.split(jax.random.fold_in(key, 7), 3)
    upper = MEMBERS // 8 + 1
    fours = jax.random.randint(key_one, (), 1, upper).astype(jnp.int32)
    twos = jax.random.randint(key_two, (), 1, upper).astype(jnp.int32)
    singles = MEMBERS - 4 * fours - 2 * twos
    shuffle = jax.random.permutation(key_three, MEMBERS).astype(jnp.int32)
    ranks = jnp.zeros((MEMBERS,), jnp.int32).at[shuffle].set(jnp.arange(MEMBERS, dtype=jnp.int32))
    result = jnp.where(ranks < fours, 4, jnp.where(ranks < fours + twos, 2, jnp.where(ranks < fours + twos + singles, 1, 0)))
    return result.astype(jnp.int32)


def shard_levels(rng, shape, cuts, low, top_value):
    factor_of, own = 1.0, jax.random.fold_in(rng, 6)
    for axis_at, blocks in cuts:
        heights = jnp.exp(jax.random.uniform(jax.random.fold_in(own, axis_at), (blocks,), jnp.float32, low / len(cuts), top_value / len(cuts)))
        factor_of = factor_of * jnp.repeat(heights, shape[axis_at] // blocks).reshape([-1 if axis == axis_at else 1 for axis in range(len(shape))])
    return factor_of


def centred(stream_key, dims, width, bound, cuts=(), kind=jnp.bfloat16):
    loudness = shard_levels(stream_key, dims, cuts, -0.22, 0.18) if cuts else 1.0
    drawn = jax.random.normal(stream_key, dims, jnp.float32) * width * loudness
    return jnp.minimum(jnp.maximum(drawn, -bound), bound).astype(kind)


def setup_inputs(seed: int = 0) -> dict:
    key_of = jax.random.split(jax.random.key(seed), 9)
    return {
        "ensemble": centred(key_of[0], (MEMBERS, LEV, NLAT, NLON), 1.0, 4.0, ((0, 16), (2, 2)), jnp.float32),
        "counts": draw_counts(jax.random.fold_in(key_of[8], 71), 0),
        "mixing": centred(key_of[2], (LEV, LEV), LEV ** -0.5, 0.75),
        "weights": jnp.clip(0.5 + 1.0 * jax.random.uniform(key_of[3], (NLAT,), jnp.float32) ** shard_levels(key_of[3], (NLAT,), ((0, 2),), -0.2, 0.2), 0.5, 1.5),
        "legendre": centred(key_of[4], (M, NLAT, NTOT), ((NLAT + NTOT) // 2) ** -0.5, 0.5, ((0, 2),)),
        "to_modes": centred(key_of[5], (LEV, LEV), LEV ** -0.5, 0.75, (), jnp.float32),
        "from_modes": centred(key_of[6], (LEV, LEV), LEV ** -0.5, 0.75, (), jnp.float32),
        "mode_rates": jnp.clip(jnp.exp(jax.random.uniform(key_of[7], (LEV,), jnp.float32, math.log(0.1), math.log(10.0))), 0.1, 10.0),
    }


time_step = 0.3
cubic_rate = 0.1


def clone_sources(counts):
    living = (counts > 0).astype(jnp.int32)
    surplus_end = jnp.cumsum(jnp.maximum(counts - 1, 0), dtype=jnp.int32)
    killed_rank = jnp.cumsum(1 - living, dtype=jnp.int32) - (1 - living)
    pulled = jnp.sum((surplus_end[None, :] <= killed_rank[:, None]).astype(jnp.int32), axis=1, dtype=jnp.int32)
    members = jnp.arange(counts.shape[0], dtype=jnp.int32)
    return jnp.where(living > 0, members, pulled).astype(jnp.int32)


def fourier_tables(wavenumber, component, longitudes):
    positions = jnp.arange(longitudes, dtype=jnp.int32)
    product_index = (positions[:, None] * wavenumber[None, :]) % longitudes
    angles = (2.0 * math.pi / longitudes) * product_index.astype(jnp.float32)
    signed = jnp.where(component[None, :] == 0, jnp.cos(angles), -jnp.sin(angles))
    factor = jnp.where(wavenumber == 0, 1.0, 2.0).astype(jnp.float32)
    return signed.astype(jnp.bfloat16), (factor[None, :] * signed).T.astype(jnp.bfloat16)


def mode_divisor(mode_rates, degree_count):
    degrees = jnp.arange(degree_count, dtype=jnp.float32)
    degree_ratio = degrees * (degrees + 1.0) / (degree_count * (degree_count + 1.0))
    return 1.0 + mode_rates[:, None] * degree_ratio[None, :]


def widen(values):
    return lax.optimization_barrier(values).astype(jnp.float32)


def grid_section(state_grid, mixing, lat_scale, forward):
    level_count, row_count, col_count = state_grid.shape
    rounded = widen(state_grid.astype(jnp.bfloat16))
    mixing_term = jnp.dot(mixing.astype(jnp.float32), rounded.reshape(level_count, row_count * col_count),
                          precision=lax.Precision.HIGHEST).reshape(level_count, row_count, col_count)
    tendency = state_grid + time_step * (mixing_term - cubic_rate * state_grid * state_grid * state_grid)
    grid_rounded = widen(tendency.astype(jnp.bfloat16)).reshape(level_count * row_count, col_count)
    fourier_sums = jnp.dot(grid_rounded, forward.astype(jnp.float32), precision=lax.Precision.HIGHEST)
    fourier_sums = fourier_sums.reshape(level_count, row_count, forward.shape[1])
    return (fourier_sums * lat_scale[None, :, None]).astype(jnp.bfloat16)


def implicit_solve(spectral, to_modes, from_modes, divisor):
    modal = jnp.einsum("kl,pmln->pmkn", to_modes, spectral, precision=lax.Precision.HIGHEST) / divisor[None, None]
    return jnp.einsum("lk,pmkn->pmln", from_modes, modal, precision=lax.Precision.HIGHEST).astype(jnp.bfloat16)


def reference(ensemble, counts, mixing, weights, legendre, to_modes, from_modes, mode_rates):
    total_waves = legendre.shape[0]
    columns = jnp.arange(2 * total_waves, dtype=jnp.int32)
    wavenumber = columns % total_waves
    component = columns // total_waves
    forward, backward = fourier_tables(wavenumber, component, NLON)
    backward_wide = backward.astype(jnp.float32)
    lat_scale = weights / NLON
    divisor = mode_divisor(mode_rates, NTOT)
    sources = clone_sources(counts)
    legendre_wide = legendre.astype(jnp.float32)

    def advance(member_index):
        state_grid = jnp.take(ensemble, member_index, axis=0)
        for timestep in range(2):
            coefficients = grid_section(state_grid, mixing, lat_scale, forward)
            split_parts = widen(coefficients).reshape(LEV, NLAT, 2, total_waves)
            spectral = jnp.einsum("ljpm,mjn->pmln", split_parts, legendre_wide, precision=lax.Precision.HIGHEST)
            implicit = widen(implicit_solve(spectral, to_modes, from_modes, divisor))
            band_parts = jnp.einsum("mjn,pmln->ljpm", legendre_wide, implicit, precision=lax.Precision.HIGHEST)
            band_parts = widen(band_parts.astype(jnp.bfloat16)).reshape(LEV * NLAT, 2 * total_waves)
            state_grid = jnp.dot(band_parts, backward_wide, precision=lax.Precision.HIGHEST).reshape(LEV, NLAT, NLON)
        return state_grid

    return lax.map(advance, sources)
```

```python
import math

import jax
import jax.numpy as jnp
from jax import lax
from jax.sharding import PartitionSpec as P

time_step = 0.3
cubic_rate = 0.1


def clone_sources(counts):
    living = (counts > 0).astype(jnp.int32)
    surplus_end = jnp.cumsum(jnp.maximum(counts - 1, 0), dtype=jnp.int32)
    killed_rank = jnp.cumsum(1 - living, dtype=jnp.int32) - (1 - living)
    pulled = jnp.sum(
        (surplus_end[None, :] <= killed_rank[:, None]).astype(jnp.int32), axis=1, dtype=jnp.int32
    )
    members = jnp.arange(counts.shape[0], dtype=jnp.int32)
    return jnp.where(living > 0, members, pulled)


def fourier_tables(wavenumber, component, longitudes):
    positions = jnp.arange(longitudes, dtype=jnp.int32)
    product_index = positions[:, None] * wavenumber[None, :] % longitudes
    angles = 2.0 * math.pi / longitudes * product_index.astype(jnp.float32)
    signed = jnp.where(component[None, :] == 0, jnp.cos(angles), -jnp.sin(angles))
    factor = jnp.where(wavenumber == 0, 1.0, 2.0).astype(jnp.float32)
    return (signed.astype(jnp.bfloat16), (factor[None, :] * signed).T.astype(jnp.bfloat16))


def mode_divisor(mode_rates, degree_count):
    degrees = jnp.arange(degree_count, dtype=jnp.float32)
    degree_ratio = degrees * (degrees + 1.0) / (degree_count * (degree_count + 1.0))
    return 1.0 + mode_rates[:, None] * degree_ratio[None, :]


def grid_section(state_grid, mixing, lat_scale, forward):
    level_count, row_count, col_count = state_grid.shape
    rounded = state_grid.astype(jnp.bfloat16)
    mixing_term = jnp.dot(
        mixing,
        rounded.reshape(level_count, row_count * col_count),
        preferred_element_type=jnp.float32,
    ).reshape(level_count, row_count, col_count)
    tendency = state_grid + time_step * (
        mixing_term - cubic_rate * state_grid * state_grid * state_grid
    )
    grid_rounded = tendency.astype(jnp.bfloat16).reshape(level_count * row_count, col_count)
    fourier_sums = jnp.dot(grid_rounded, forward, preferred_element_type=jnp.float32)
    fourier_sums = fourier_sums.reshape(level_count, row_count, forward.shape[1])
    return (fourier_sums * lat_scale[None, :, None]).astype(jnp.bfloat16)


def implicit_solve(spectral, to_modes, from_modes, divisor):
    modal = (
        jnp.einsum("kl,pmln->pmkn", to_modes, spectral, precision=lax.Precision.HIGHEST)
        / divisor[None, None]
    )
    return jnp.einsum("lk,pmkn->pmln", from_modes, modal, precision=lax.Precision.HIGHEST).astype(
        jnp.bfloat16
    )


def local(ensemble, counts, mixing, weights, legendre, to_modes, from_modes, mode_rates):
    traj_count = lax.axis_size("traj")
    lat_count = lax.axis_size("lat")
    local_waves = legendre.shape[0]
    degree_count = legendre.shape[2]
    total_waves = local_waves * lat_count
    longitudes = ensemble.shape[3]
    columns = jnp.arange(2 * total_waves, dtype=jnp.int32)
    within = columns % (2 * local_waves)
    wavenumber = columns // (2 * local_waves) * local_waves + within % local_waves
    component = within // local_waves
    forward, backward = fourier_tables(wavenumber, component, longitudes)
    lat_scale = weights / longitudes
    divisor = mode_divisor(mode_rates, degree_count)
    sources = clone_sources(lax.all_gather(counts, "traj", axis=0, tiled=True))

    def to_spectral(received):
        split_parts = received.reshape(received.shape[0], received.shape[1], 2, local_waves)
        return jnp.einsum(
            "ljpm,mjn->pmln", split_parts, legendre, preferred_element_type=jnp.float32
        )

    def to_grid(received):
        flat_rows = received.reshape(received.shape[0] * received.shape[1], received.shape[2])
        result_grid = jnp.dot(flat_rows, backward, preferred_element_type=jnp.float32)
        return result_grid.reshape(received.shape[0], received.shape[1], longitudes)

    def to_implicit(coefficients):
        spectral = to_spectral(
            lax.all_to_all(coefficients, "lat", split_axis=2, concat_axis=1, tiled=True)
        )
        return implicit_solve(spectral, to_modes, from_modes, divisor)

    def clone(implicit):
        pieces = implicit.reshape(traj_count, -1, degree_count)
        spread = lax.all_to_all(pieces, "traj", split_axis=0, concat_axis=0, tiled=True)
        chosen = jnp.take(spread, sources, axis=0)
        merged = lax.all_to_all(chosen, "traj", split_axis=0, concat_axis=0, tiled=True)
        return merged.reshape(implicit.shape)

    def to_band_grid(implicit):
        band_parts = jnp.einsum(
            "mjn,pmln->ljpm", legendre, implicit, preferred_element_type=jnp.float32
        )
        band_parts = band_parts.astype(jnp.bfloat16)
        band_parts = band_parts.reshape(band_parts.shape[0], band_parts.shape[1], 2 * local_waves)
        return to_grid(lax.all_to_all(band_parts, "lat", split_axis=1, concat_axis=2, tiled=True))

    state_grid = ensemble[0]
    implicit = clone(to_implicit(grid_section(state_grid, mixing, lat_scale, forward)))
    state_grid = to_band_grid(implicit)
    state_grid = to_band_grid(to_implicit(grid_section(state_grid, mixing, lat_scale, forward)))
    return state_grid[None]


def solution(mesh):
    placed = (
        P("traj", None, "lat", None),
        P("traj"),
        P(),
        P("lat"),
        P("lat", None, None),
        P(),
        P(),
        P(),
    )
    return jax.shard_map(
        local, mesh=mesh, in_specs=placed, out_specs=P("traj", None, "lat", None), check_vma=False
    )
```

```python
import math

import jax
import jax.numpy as jnp
from jax import lax
from jax.experimental import pallas as pl
from jax.experimental.pallas import tpu as pltpu
from jax.sharding import PartitionSpec as P

time_step = 0.3
cubic_rate = 0.1


def clone_sources(counts):
    living = (counts > 0).astype(jnp.int32)
    surplus_end = jnp.cumsum(jnp.maximum(counts - 1, 0), dtype=jnp.int32)
    killed_rank = jnp.cumsum(1 - living, dtype=jnp.int32) - (1 - living)
    pulled = jnp.sum(
        (surplus_end[None, :] <= killed_rank[:, None]).astype(jnp.int32), axis=1, dtype=jnp.int32
    )
    members = jnp.arange(counts.shape[0], dtype=jnp.int32)
    return jnp.where(living > 0, members, pulled)


def fourier_tables(wavenumber, component, longitudes):
    positions = jnp.arange(longitudes, dtype=jnp.int32)
    product_index = positions[:, None] * wavenumber[None, :] % longitudes
    angles = 2.0 * math.pi / longitudes * product_index.astype(jnp.float32)
    signed = jnp.where(component[None, :] == 0, jnp.cos(angles), -jnp.sin(angles))
    factor = jnp.where(wavenumber == 0, 1.0, 2.0).astype(jnp.float32)
    return (signed.astype(jnp.bfloat16), (factor[None, :] * signed).T.astype(jnp.bfloat16))


def mode_divisor(mode_rates, degree_count):
    degrees = jnp.arange(degree_count, dtype=jnp.float32)
    degree_ratio = degrees * (degrees + 1.0) / (degree_count * (degree_count + 1.0))
    return 1.0 + mode_rates[:, None] * degree_ratio[None, :]


def grid_section(state_grid, mixing, lat_scale, forward):
    level_count, row_count, col_count = state_grid.shape
    rounded = state_grid.astype(jnp.bfloat16)
    mixing_term = jnp.dot(
        mixing,
        rounded.reshape(level_count, row_count * col_count),
        preferred_element_type=jnp.float32,
    ).reshape(level_count, row_count, col_count)
    tendency = state_grid + time_step * (
        mixing_term - cubic_rate * state_grid * state_grid * state_grid
    )
    grid_rounded = tendency.astype(jnp.bfloat16).reshape(level_count * row_count, col_count)
    fourier_sums = jnp.dot(grid_rounded, forward, preferred_element_type=jnp.float32)
    fourier_sums = fourier_sums.reshape(level_count, row_count, forward.shape[1])
    return (fourier_sums * lat_scale[None, :, None]).astype(jnp.bfloat16)


def implicit_solve(spectral, to_modes, from_modes, divisor):
    modal = (
        jnp.einsum("kl,pmln->pmkn", to_modes, spectral, precision=lax.Precision.HIGHEST)
        / divisor[None, None]
    )
    return jnp.einsum("lk,pmkn->pmln", from_modes, modal, precision=lax.Precision.HIGHEST).astype(
        jnp.bfloat16
    )


def spread_mixing(mixing):
    return jnp.kron(mixing, jnp.eye(8, dtype=mixing.dtype))


def to_coefficients(values, mixer, scale, forward):
    level_count, rows, longitudes = values.shape
    flat = values.reshape(level_count * rows, longitudes)
    mixed = jnp.dot(mixer, flat.astype(jnp.bfloat16), preferred_element_type=jnp.float32)
    tendency = flat + time_step * (mixed - cubic_rate * flat * flat * flat)
    sums = jnp.dot(tendency.astype(jnp.bfloat16), forward, preferred_element_type=jnp.float32)
    return sums.reshape(level_count, rows, forward.shape[1]) * scale[None, :, :1]


def from_bands(bands, backward):
    parts, level_count, rows, width = bands.shape
    total = None
    for part in range(parts):
        term = jnp.dot(
            bands[part].astype(jnp.bfloat16).reshape(level_count * rows, width),
            backward[part * width : (part + 1) * width, :],
            preferred_element_type=jnp.float32,
        )
        total = term if total is None else total + term
    return total.reshape(level_count, rows, backward.shape[1])


def split_columns(pieces, out_ref):
    whole = jnp.concatenate(pieces, axis=1)
    width = out_ref.shape[3]
    for part in range(out_ref.shape[0]):
        out_ref[part] = whole[:, :, part * width : (part + 1) * width].astype(jnp.bfloat16)


def first_kernel(grid_ref, mixer_ref, scale_ref, forward_ref, out_ref):
    pieces = []
    for low in range(0, grid_ref.shape[1], 8):
        values = grid_ref[:, low : low + 8, :]
        scale = scale_ref[low : low + 8, :]
        pieces.append(to_coefficients(values, mixer_ref[...], scale, forward_ref[...]))
    split_columns(pieces, out_ref)


def middle_kernel(bands_ref, backward_ref, mixer_ref, scale_ref, forward_ref, out_ref):
    whole = from_bands(bands_ref[...], backward_ref[...])
    pieces = []
    for low in range(0, whole.shape[1], 8):
        scale = scale_ref[low : low + 8, :]
        values = whole[:, low : low + 8, :]
        pieces.append(to_coefficients(values, mixer_ref[...], scale, forward_ref[...]))
    split_columns(pieces, out_ref)


def last_kernel(bands_ref, backward_ref, out_ref):
    out_ref[...] = from_bands(bands_ref[...], backward_ref[...])


def fixed(array):
    return pl.BlockSpec(array.shape, lambda step: (0,) * array.ndim)


def by_rows(shape, axis, block):
    sizes = tuple(block if at == axis else size for at, size in enumerate(shape))
    return pl.BlockSpec(sizes, lambda step: tuple(step if at == axis else 0 for at in range(len(shape))))


def row_call(kernel, operands, row_axes, out_shape, out_axis, out_type, block):
    rows = out_shape[out_axis]
    specs = [
        fixed(op) if axis is None else by_rows(op.shape, axis, block)
        for op, axis in zip(operands, row_axes)
    ]
    return pl.pallas_call(
        kernel,
        grid=(rows // block,),
        in_specs=specs,
        out_specs=by_rows(out_shape, out_axis, block),
        out_shape=jax.ShapeDtypeStruct(out_shape, out_type),
        compiler_params=pltpu.CompilerParams(vmem_limit_bytes=40 * 1024 * 1024),
    )(*operands)


def local(ensemble, counts, mixing, weights, legendre, to_modes, from_modes, mode_rates):
    traj_count = lax.axis_size("traj")
    lat_count = lax.axis_size("lat")
    local_waves = legendre.shape[0]
    degree_count = legendre.shape[2]
    total_waves = local_waves * lat_count
    longitudes = ensemble.shape[3]
    columns = jnp.arange(2 * total_waves, dtype=jnp.int32)
    within = columns % (2 * local_waves)
    wavenumber = columns // (2 * local_waves) * local_waves + within % local_waves
    component = within // local_waves
    forward, backward = fourier_tables(wavenumber, component, longitudes)
    lat_scale = weights / longitudes
    divisor = mode_divisor(mode_rates, degree_count)
    sources = clone_sources(lax.all_gather(counts, "traj", axis=0, tiled=True))

    def to_spectral(received):
        split_parts = received.reshape(received.shape[0], received.shape[1], 2, local_waves)
        return jnp.einsum(
            "ljpm,mjn->pmln", split_parts, legendre, preferred_element_type=jnp.float32
        )

    def to_grid(received):
        flat_rows = received.reshape(received.shape[0] * received.shape[1], received.shape[2])
        result_grid = jnp.dot(flat_rows, backward, preferred_element_type=jnp.float32)
        return result_grid.reshape(received.shape[0], received.shape[1], longitudes)

    def to_implicit(coefficients):
        spectral = to_spectral(
            lax.all_to_all(coefficients, "lat", split_axis=2, concat_axis=1, tiled=True)
        )
        return implicit_solve(spectral, to_modes, from_modes, divisor)

    def clone(implicit):
        pieces = implicit.reshape(traj_count, -1, degree_count)
        spread = lax.all_to_all(pieces, "traj", split_axis=0, concat_axis=0, tiled=True)
        chosen = jnp.take(spread, sources, axis=0)
        merged = lax.all_to_all(chosen, "traj", split_axis=0, concat_axis=0, tiled=True)
        return merged.reshape(implicit.shape)

    def to_band_grid(implicit):
        band_parts = jnp.einsum(
            "mjn,pmln->ljpm", legendre, implicit, preferred_element_type=jnp.float32
        )
        band_parts = band_parts.astype(jnp.bfloat16)
        band_parts = band_parts.reshape(band_parts.shape[0], band_parts.shape[1], 2 * local_waves)
        return to_grid(lax.all_to_all(band_parts, "lat", split_axis=1, concat_axis=2, tiled=True))

    state_grid = ensemble[0]
    level_count, row_count, col_count = state_grid.shape
    width = 2 * local_waves
    block = 16
    if width % 128 or row_count % block:
        implicit = clone(to_implicit(grid_section(state_grid, mixing, lat_scale, forward)))
        state_grid = to_band_grid(implicit)
        state_grid = to_band_grid(
            to_implicit(grid_section(state_grid, mixing, lat_scale, forward))
        )
        return state_grid[None]

    mixer = spread_mixing(mixing)
    scale = jnp.broadcast_to(lat_scale[:, None], (row_count, 128))
    coeff_shape = (lat_count, level_count, row_count, width)

    def swap(blocks):
        return lax.all_to_all(blocks, "lat", split_axis=0, concat_axis=0, tiled=True)

    def solve(blocks):
        rows = blocks.transpose(1, 0, 2, 3).reshape(level_count, lat_count * row_count, width)
        return implicit_solve(to_spectral(rows), to_modes, from_modes, divisor)

    def bands_of(implicit):
        band_parts = jnp.einsum(
            "mjn,pmln->ljpm", legendre, implicit, preferred_element_type=jnp.float32
        ).astype(jnp.bfloat16)
        band_parts = band_parts.reshape(level_count, lat_count, row_count, width)
        return band_parts.transpose(1, 0, 2, 3)

    coefficients = row_call(
        first_kernel,
        (state_grid, mixer, scale, forward),
        (1, None, 0, None),
        coeff_shape,
        2,
        jnp.bfloat16,
        block,
    )
    bands = swap(bands_of(clone(solve(swap(coefficients)))))
    coefficients = row_call(
        middle_kernel,
        (bands, backward, mixer, scale, forward),
        (2, None, None, 0, None),
        coeff_shape,
        2,
        jnp.bfloat16,
        block,
    )
    bands = swap(bands_of(solve(swap(coefficients))))
    state_grid = row_call(
        last_kernel,
        (bands, backward),
        (2, None),
        state_grid.shape,
        1,
        jnp.float32,
        block,
    )
    return state_grid[None]


def solution(mesh):
    placed = (
        P("traj", None, "lat", None),
        P("traj"),
        P(),
        P("lat"),
        P("lat", None, None),
        P(),
        P(),
        P(),
    )
    return jax.shard_map(
        local, mesh=mesh, in_specs=placed, out_specs=P("traj", None, "lat", None), check_vma=False
    )
```

```python
import math

import jax
import jax.numpy as jnp
from jax import lax
from jax.experimental import pallas as pl
from jax.experimental.pallas import tpu as pltpu
from jax.sharding import PartitionSpec as P

time_step = 0.3
cubic_rate = 0.1


def clone_sources(counts):
    living = (counts > 0).astype(jnp.int32)
    surplus_end = jnp.cumsum(jnp.maximum(counts - 1, 0), dtype=jnp.int32)
    killed_rank = jnp.cumsum(1 - living, dtype=jnp.int32) - (1 - living)
    pulled = jnp.sum(
        (surplus_end[None, :] <= killed_rank[:, None]).astype(jnp.int32), axis=1, dtype=jnp.int32
    )
    members = jnp.arange(counts.shape[0], dtype=jnp.int32)
    return jnp.where(living > 0, members, pulled)


def fourier_tables(wavenumber, component, longitudes):
    positions = jnp.arange(longitudes, dtype=jnp.int32)
    product_index = positions[:, None] * wavenumber[None, :] % longitudes
    angles = 2.0 * math.pi / longitudes * product_index.astype(jnp.float32)
    signed = jnp.where(component[None, :] == 0, jnp.cos(angles), -jnp.sin(angles))
    factor = jnp.where(wavenumber == 0, 1.0, 2.0).astype(jnp.float32)
    return (signed.astype(jnp.bfloat16), (factor[None, :] * signed).T.astype(jnp.bfloat16))


def mode_divisor(mode_rates, degree_count):
    degrees = jnp.arange(degree_count, dtype=jnp.float32)
    degree_ratio = degrees * (degrees + 1.0) / (degree_count * (degree_count + 1.0))
    return 1.0 + mode_rates[:, None] * degree_ratio[None, :]


def grid_section(state_grid, mixing, lat_scale, forward):
    level_count, row_count, col_count = state_grid.shape
    rounded = state_grid.astype(jnp.bfloat16)
    mixing_term = jnp.dot(
        mixing,
        rounded.reshape(level_count, row_count * col_count),
        preferred_element_type=jnp.float32,
    ).reshape(level_count, row_count, col_count)
    tendency = state_grid + time_step * (
        mixing_term - cubic_rate * state_grid * state_grid * state_grid
    )
    grid_rounded = tendency.astype(jnp.bfloat16).reshape(level_count * row_count, col_count)
    fourier_sums = jnp.dot(grid_rounded, forward, preferred_element_type=jnp.float32)
    fourier_sums = fourier_sums.reshape(level_count, row_count, forward.shape[1])
    return (fourier_sums * lat_scale[None, :, None]).astype(jnp.bfloat16)


def implicit_solve(spectral, to_modes, from_modes, divisor):
    modal = (
        jnp.einsum("kl,pmln->pmkn", to_modes, spectral, precision=lax.Precision.HIGHEST)
        / divisor[None, None]
    )
    return jnp.einsum("lk,pmkn->pmln", from_modes, modal, precision=lax.Precision.HIGHEST).astype(
        jnp.bfloat16
    )


def spread_mixing(mixing):
    level_count = mixing.shape[0]
    at = jnp.arange(8 * level_count, dtype=jnp.int32)
    picks = (at[:, None] // 8 == jnp.arange(level_count)[None, :]).astype(mixing.dtype)
    tall = jnp.dot(picks, mixing, preferred_element_type=jnp.float32).astype(mixing.dtype)
    both = jnp.dot(tall, picks.T, preferred_element_type=jnp.float32)
    same_row = at[:, None] % 8 == at[None, :] % 8
    return jnp.where(same_row, both, 0.0).astype(mixing.dtype)


def to_coefficients(values, mixer, scale, forward):
    level_count, rows, longitudes = values.shape
    flat = values.reshape(level_count * rows, longitudes)
    mixed = jnp.dot(mixer, flat.astype(jnp.bfloat16), preferred_element_type=jnp.float32)
    tendency = flat + time_step * (mixed - cubic_rate * flat * flat * flat)
    sums = jnp.dot(tendency.astype(jnp.bfloat16), forward, preferred_element_type=jnp.float32)
    return sums.reshape(level_count, rows, forward.shape[1]) * scale[None, :, :1]


def from_bands(bands, backward):
    parts, level_count, rows, width = bands.shape
    total = None
    for part in range(parts):
        term = jnp.dot(
            bands[part].astype(jnp.bfloat16).reshape(level_count * rows, width),
            backward[part * width : (part + 1) * width, :],
            preferred_element_type=jnp.float32,
        )
        total = term if total is None else total + term
    return total.reshape(level_count, rows, backward.shape[1])


def split_columns(pieces, out_ref):
    whole = jnp.concatenate(pieces, axis=1)
    width = out_ref.shape[3]
    for part in range(out_ref.shape[0]):
        out_ref[part] = whole[:, :, part * width : (part + 1) * width].astype(jnp.bfloat16)


def first_kernel(grid_ref, mixer_ref, scale_ref, forward_ref, out_ref):
    pieces = []
    for low in range(0, grid_ref.shape[1], 8):
        values = grid_ref[:, low : low + 8, :]
        scale = scale_ref[low : low + 8, :]
        pieces.append(to_coefficients(values, mixer_ref[...], scale, forward_ref[...]))
    split_columns(pieces, out_ref)


def middle_kernel(bands_ref, backward_ref, mixer_ref, scale_ref, forward_ref, out_ref):
    whole = from_bands(bands_ref[...], backward_ref[...])
    pieces = []
    for low in range(0, whole.shape[1], 8):
        scale = scale_ref[low : low + 8, :]
        values = whole[:, low : low + 8, :]
        pieces.append(to_coefficients(values, mixer_ref[...], scale, forward_ref[...]))
    split_columns(pieces, out_ref)


def last_kernel(bands_ref, backward_ref, out_ref):
    out_ref[...] = from_bands(bands_ref[...], backward_ref[...])


def fixed(array):
    return pl.BlockSpec(array.shape, lambda step: (0,) * array.ndim)


def by_rows(shape, axis, block):
    sizes = tuple(block if at == axis else size for at, size in enumerate(shape))
    return pl.BlockSpec(sizes, lambda step: tuple(step if at == axis else 0 for at in range(len(shape))))


def row_call(kernel, operands, row_axes, out_shape, out_axis, out_type, block):
    rows = out_shape[out_axis]
    specs = [
        fixed(op) if axis is None else by_rows(op.shape, axis, block)
        for op, axis in zip(operands, row_axes)
    ]
    return pl.pallas_call(
        kernel,
        grid=(rows // block,),
        in_specs=specs,
        out_specs=by_rows(out_shape, out_axis, block),
        out_shape=jax.ShapeDtypeStruct(out_shape, out_type),
        compiler_params=pltpu.CompilerParams(vmem_limit_bytes=40 * 1024 * 1024),
    )(*operands)


def local(ensemble, counts, mixing, weights, legendre, to_modes, from_modes, mode_rates):
    traj_count = lax.axis_size("traj")
    lat_count = lax.axis_size("lat")
    local_waves = legendre.shape[0]
    degree_count = legendre.shape[2]
    total_waves = local_waves * lat_count
    longitudes = ensemble.shape[3]
    columns = jnp.arange(2 * total_waves, dtype=jnp.int32)
    within = columns % (2 * local_waves)
    width = 2 * local_waves
    block = 16
    whole_blocks = width % 128 == 0 and ensemble.shape[2] % block == 0
    if whole_blocks:
        wave_of, component = within // 2, within % 2
    else:
        wave_of, component = within % local_waves, within // local_waves
    wavenumber = columns // width * local_waves + wave_of
    forward, backward = fourier_tables(wavenumber, component, longitudes)
    lat_scale = weights / longitudes
    divisor = mode_divisor(mode_rates, degree_count)
    sources = clone_sources(lax.all_gather(counts, "traj", axis=0, tiled=True))

    def to_spectral(received):
        split_parts = received.reshape(received.shape[0], received.shape[1], 2, local_waves)
        return jnp.einsum(
            "ljpm,mjn->pmln", split_parts, legendre, preferred_element_type=jnp.float32
        )

    def to_grid(received):
        flat_rows = received.reshape(received.shape[0] * received.shape[1], received.shape[2])
        result_grid = jnp.dot(flat_rows, backward, preferred_element_type=jnp.float32)
        return result_grid.reshape(received.shape[0], received.shape[1], longitudes)

    def to_implicit(coefficients):
        spectral = to_spectral(
            lax.all_to_all(coefficients, "lat", split_axis=2, concat_axis=1, tiled=True)
        )
        return implicit_solve(spectral, to_modes, from_modes, divisor)

    def clone(implicit):
        pieces = implicit.reshape(traj_count, -1, degree_count)
        spread = lax.all_to_all(pieces, "traj", split_axis=0, concat_axis=0, tiled=True)
        chosen = jnp.take(spread, sources, axis=0)
        merged = lax.all_to_all(chosen, "traj", split_axis=0, concat_axis=0, tiled=True)
        return merged.reshape(implicit.shape)

    def to_band_grid(implicit):
        band_parts = jnp.einsum(
            "mjn,pmln->ljpm", legendre, implicit, preferred_element_type=jnp.float32
        )
        band_parts = band_parts.astype(jnp.bfloat16)
        band_parts = band_parts.reshape(band_parts.shape[0], band_parts.shape[1], 2 * local_waves)
        return to_grid(lax.all_to_all(band_parts, "lat", split_axis=1, concat_axis=2, tiled=True))

    state_grid = ensemble[0]
    level_count, row_count, col_count = state_grid.shape
    if not whole_blocks:
        implicit = clone(to_implicit(grid_section(state_grid, mixing, lat_scale, forward)))
        state_grid = to_band_grid(implicit)
        state_grid = to_band_grid(
            to_implicit(grid_section(state_grid, mixing, lat_scale, forward))
        )
        return state_grid[None]

    mixer = spread_mixing(mixing)
    scale = jnp.broadcast_to(lat_scale[:, None], (row_count, 128))
    coeff_shape = (lat_count, level_count, row_count, width)

    def swap(blocks):
        return lax.all_to_all(blocks, "lat", split_axis=0, concat_axis=0, tiled=True)

    tables = legendre.reshape(local_waves, lat_count, row_count, degree_count)

    def solve(blocks):
        columns_first = lax.optimization_barrier(blocks.transpose(0, 3, 1, 2))
        rows = columns_first.reshape(lat_count, local_waves, 2 * level_count, row_count)
        spectral = sum(
            jnp.einsum(
                "mrj,mjn->mrn", rows[part], tables[:, part], preferred_element_type=jnp.float32
            )
            for part in range(lat_count)
        )
        spectral = spectral.reshape(1, width, level_count, degree_count)
        return implicit_solve(spectral, to_modes, from_modes, divisor)

    def bands_of(implicit):
        rows = implicit.reshape(local_waves, 2 * level_count, degree_count)
        parts = [
            jnp.einsum(
                "mrn,mjn->mrj", rows, tables[:, part], preferred_element_type=jnp.float32
            ).astype(jnp.bfloat16)
            for part in range(lat_count)
        ]
        columns_first = jnp.stack(parts).reshape(lat_count, width, level_count, row_count)
        return lax.optimization_barrier(columns_first).transpose(0, 2, 3, 1)

    coefficients = row_call(
        first_kernel,
        (state_grid, mixer, scale, forward),
        (1, None, 0, None),
        coeff_shape,
        2,
        jnp.bfloat16,
        block,
    )
    bands = swap(bands_of(clone(solve(swap(coefficients)))))
    coefficients = row_call(
        middle_kernel,
        (bands, backward, mixer, scale, forward),
        (2, None, None, 0, None),
        coeff_shape,
        2,
        jnp.bfloat16,
        block,
    )
    bands = swap(bands_of(solve(swap(coefficients))))
    state_grid = row_call(
        last_kernel,
        (bands, backward),
        (2, None),
        state_grid.shape,
        1,
        jnp.float32,
        block,
    )
    return state_grid[None]


def solution(mesh):
    placed = (
        P("traj", None, "lat", None),
        P("traj"),
        P(),
        P("lat"),
        P("lat", None, None),
        P(),
        P(),
        P(),
    )
    return jax.shard_map(
        local, mesh=mesh, in_specs=placed, out_specs=P("traj", None, "lat", None), check_vma=False
    )
```

```python
import functools
import math

import jax
import jax.numpy as jnp
from jax import lax
from jax.experimental import pallas as pl
from jax.experimental.pallas import tpu as pltpu
from jax.sharding import PartitionSpec as P

time_step = 0.3
cubic_rate = 0.1


def clone_sources(counts):
    living = (counts > 0).astype(jnp.int32)
    surplus_end = jnp.cumsum(jnp.maximum(counts - 1, 0), dtype=jnp.int32)
    killed_rank = jnp.cumsum(1 - living, dtype=jnp.int32) - (1 - living)
    pulled = jnp.sum(
        (surplus_end[None, :] <= killed_rank[:, None]).astype(jnp.int32), axis=1, dtype=jnp.int32
    )
    members = jnp.arange(counts.shape[0], dtype=jnp.int32)
    return jnp.where(living > 0, members, pulled)


def fourier_tables(wavenumber, component, longitudes):
    positions = jnp.arange(longitudes, dtype=jnp.int32)
    product_index = positions[:, None] * wavenumber[None, :] % longitudes
    angles = 2.0 * math.pi / longitudes * product_index.astype(jnp.float32)
    signed = jnp.where(component[None, :] == 0, jnp.cos(angles), -jnp.sin(angles))
    factor = jnp.where(wavenumber == 0, 1.0, 2.0).astype(jnp.float32)
    return (signed.astype(jnp.bfloat16), (factor[None, :] * signed).T.astype(jnp.bfloat16))


def mode_divisor(mode_rates, degree_count):
    degrees = jnp.arange(degree_count, dtype=jnp.float32)
    degree_ratio = degrees * (degrees + 1.0) / (degree_count * (degree_count + 1.0))
    return 1.0 + mode_rates[:, None] * degree_ratio[None, :]


def grid_section(state_grid, mixing, lat_scale, forward):
    level_count, row_count, col_count = state_grid.shape
    rounded = state_grid.astype(jnp.bfloat16)
    mixing_term = jnp.dot(
        mixing,
        rounded.reshape(level_count, row_count * col_count),
        preferred_element_type=jnp.float32,
    ).reshape(level_count, row_count, col_count)
    tendency = state_grid + time_step * (
        mixing_term - cubic_rate * state_grid * state_grid * state_grid
    )
    grid_rounded = tendency.astype(jnp.bfloat16).reshape(level_count * row_count, col_count)
    fourier_sums = jnp.dot(grid_rounded, forward, preferred_element_type=jnp.float32)
    fourier_sums = fourier_sums.reshape(level_count, row_count, forward.shape[1])
    return (fourier_sums * lat_scale[None, :, None]).astype(jnp.bfloat16)


def implicit_solve(spectral, to_modes, from_modes, divisor):
    modal = (
        jnp.einsum("kl,pmln->pmkn", to_modes, spectral, precision=lax.Precision.HIGHEST)
        / divisor[None, None]
    )
    return jnp.einsum("lk,pmkn->pmln", from_modes, modal, precision=lax.Precision.HIGHEST).astype(
        jnp.bfloat16
    )


def spread_mixing(mixing):
    level_count = mixing.shape[0]
    at = jnp.arange(8 * level_count, dtype=jnp.int32)
    picks = (at[:, None] // 8 == jnp.arange(level_count)[None, :]).astype(mixing.dtype)
    tall = jnp.dot(picks, mixing, preferred_element_type=jnp.float32).astype(mixing.dtype)
    both = jnp.dot(tall, picks.T, preferred_element_type=jnp.float32)
    same_row = at[:, None] % 8 == at[None, :] % 8
    return jnp.where(same_row, both, 0.0).astype(mixing.dtype)


def to_coefficients(values, mixer, scale, forward):
    level_count, rows, longitudes = values.shape
    flat = values.reshape(level_count * rows, longitudes)
    mixed = jnp.dot(mixer, flat.astype(jnp.bfloat16), preferred_element_type=jnp.float32)
    tendency = flat + time_step * (mixed - cubic_rate * flat * flat * flat)
    sums = jnp.dot(tendency.astype(jnp.bfloat16), forward, preferred_element_type=jnp.float32)
    return sums.reshape(level_count, rows, forward.shape[1]) * scale[None, :, :1]


def from_bands(bands, backward):
    level_count, rows, width = bands[0].shape
    total = None
    for part, band in enumerate(bands):
        term = jnp.dot(
            band[...].reshape(level_count * rows, width),
            backward[part * width : (part + 1) * width, :],
            preferred_element_type=jnp.float32,
        )
        total = term if total is None else total + term
    return total.reshape(level_count, rows, backward.shape[1])


def split_columns(pieces, out_refs):
    whole = jnp.concatenate(pieces, axis=1)
    width = out_refs[0].shape[2]
    for part, out_ref in enumerate(out_refs):
        out_ref[...] = whole[:, :, part * width : (part + 1) * width].astype(jnp.bfloat16)


def first_kernel(grid_ref, mixer_ref, scale_ref, forward_ref, *out_refs):
    pieces = []
    for low in range(0, grid_ref.shape[1], 8):
        values = grid_ref[:, low : low + 8, :]
        scale = scale_ref[low : low + 8, :]
        pieces.append(to_coefficients(values, mixer_ref[...], scale, forward_ref[...]))
    split_columns(pieces, out_refs)


def middle_kernel(parts, backward_ref, mixer_ref, scale_ref, forward_ref, *refs):
    out_refs = refs[parts:]
    whole = from_bands(refs[:parts], backward_ref[...])
    pieces = []
    for low in range(0, whole.shape[1], 8):
        scale = scale_ref[low : low + 8, :]
        values = whole[:, low : low + 8, :]
        pieces.append(to_coefficients(values, mixer_ref[...], scale, forward_ref[...]))
    split_columns(pieces, out_refs)


def last_kernel(backward_ref, *refs):
    refs[-1][...] = from_bands(refs[:-1], backward_ref[...])


def fixed(array):
    return pl.BlockSpec(array.shape, lambda step: (0,) * array.ndim)


def by_rows(shape, axis, block):
    sizes = tuple(block if at == axis else size for at, size in enumerate(shape))
    return pl.BlockSpec(sizes, lambda step: tuple(step if at == axis else 0 for at in range(len(shape))))


def row_call(kernel, operands, row_axes, out_shape, out_count, out_type, block):
    rows = out_shape[1]
    specs = [
        fixed(op) if axis is None else by_rows(op.shape, axis, block)
        for op, axis in zip(operands, row_axes)
    ]
    return pl.pallas_call(
        kernel,
        grid=(rows // block,),
        in_specs=specs,
        out_specs=[by_rows(out_shape, 1, block)] * out_count,
        out_shape=[jax.ShapeDtypeStruct(out_shape, out_type)] * out_count,
        compiler_params=pltpu.CompilerParams(vmem_limit_bytes=40 * 1024 * 1024),
    )(*operands)


def local(ensemble, counts, mixing, weights, legendre, to_modes, from_modes, mode_rates):
    traj_count = lax.axis_size("traj")
    lat_count = lax.axis_size("lat")
    local_waves = legendre.shape[0]
    degree_count = legendre.shape[2]
    total_waves = local_waves * lat_count
    longitudes = ensemble.shape[3]
    columns = jnp.arange(2 * total_waves, dtype=jnp.int32)
    within = columns % (2 * local_waves)
    width = 2 * local_waves
    block = 16
    whole_blocks = width % 128 == 0 and ensemble.shape[2] % block == 0
    if whole_blocks:
        wave_of, component = within // 2, within % 2
    else:
        wave_of, component = within % local_waves, within // local_waves
    wavenumber = columns // width * local_waves + wave_of
    forward, backward = fourier_tables(wavenumber, component, longitudes)
    lat_scale = weights / longitudes
    divisor = mode_divisor(mode_rates, degree_count)
    sources = clone_sources(lax.all_gather(counts, "traj", axis=0, tiled=True))

    def to_spectral(received):
        split_parts = received.reshape(received.shape[0], received.shape[1], 2, local_waves)
        return jnp.einsum(
            "ljpm,mjn->pmln", split_parts, legendre, preferred_element_type=jnp.float32
        )

    def to_grid(received):
        flat_rows = received.reshape(received.shape[0] * received.shape[1], received.shape[2])
        result_grid = jnp.dot(flat_rows, backward, preferred_element_type=jnp.float32)
        return result_grid.reshape(received.shape[0], received.shape[1], longitudes)

    def to_implicit(coefficients):
        spectral = to_spectral(
            lax.all_to_all(coefficients, "lat", split_axis=2, concat_axis=1, tiled=True)
        )
        return implicit_solve(spectral, to_modes, from_modes, divisor)

    def clone(implicit):
        pieces = implicit.reshape(traj_count, -1, degree_count)
        spread = lax.all_to_all(pieces, "traj", split_axis=0, concat_axis=0, tiled=True)
        chosen = jnp.take(spread, sources, axis=0)
        merged = lax.all_to_all(chosen, "traj", split_axis=0, concat_axis=0, tiled=True)
        return merged.reshape(implicit.shape)

    def to_band_grid(implicit):
        band_parts = jnp.einsum(
            "mjn,pmln->ljpm", legendre, implicit, preferred_element_type=jnp.float32
        )
        band_parts = band_parts.astype(jnp.bfloat16)
        band_parts = band_parts.reshape(band_parts.shape[0], band_parts.shape[1], 2 * local_waves)
        return to_grid(lax.all_to_all(band_parts, "lat", split_axis=1, concat_axis=2, tiled=True))

    state_grid = ensemble[0]
    level_count, row_count, col_count = state_grid.shape
    if not whole_blocks:
        implicit = clone(to_implicit(grid_section(state_grid, mixing, lat_scale, forward)))
        state_grid = to_band_grid(implicit)
        state_grid = to_band_grid(
            to_implicit(grid_section(state_grid, mixing, lat_scale, forward))
        )
        return state_grid[None]

    mixer = spread_mixing(mixing)
    scale = jnp.broadcast_to(lat_scale[:, None], (row_count, 128))
    coeff_shape = (level_count, row_count, width)
    me = lax.axis_index("lat")
    shifts = range(lat_count)
    tables = legendre.reshape(local_waves, lat_count, row_count, degree_count)

    def take(array, part, axis):
        return lax.dynamic_index_in_dim(array, part % lat_count, axis, keepdims=False)

    send_tables = [take(tables, me + shift, 1) for shift in shifts]
    recv_tables = [take(tables, me - shift + lat_count, 1) for shift in shifts]
    forward_parts = forward.reshape(longitudes, lat_count, width)
    forward = jnp.concatenate([take(forward_parts, me + shift, 1) for shift in shifts], axis=1)
    backward_parts = backward.reshape(lat_count, width, longitudes)
    backward = jnp.concatenate(
        [take(backward_parts, me - shift + lat_count, 0) for shift in shifts], axis=0
    )

    def send(array, shift):
        if shift == 0:
            return array
        pairs = [(at, (at + shift) % lat_count) for at in range(lat_count)]
        return lax.ppermute(array, "lat", pairs)

    def solve(blocks):
        spectral = 0.0
        for shift in shifts:
            arrived = send(blocks[shift], shift)
            rows = lax.optimization_barrier(arrived.transpose(2, 0, 1))
            rows = rows.reshape(local_waves, 2 * level_count, row_count)
            spectral += jnp.einsum(
                "mrj,mjn->mrn", rows, recv_tables[shift], preferred_element_type=jnp.float32
            )
        spectral = spectral.reshape(1, width, level_count, degree_count)
        return implicit_solve(spectral, to_modes, from_modes, divisor)

    def bands_of(implicit):
        rows = implicit.reshape(local_waves, 2 * level_count, degree_count)
        result = []
        for shift in shifts:
            part = jnp.einsum(
                "mrn,mjn->mrj", rows, send_tables[shift], preferred_element_type=jnp.float32
            ).astype(jnp.bfloat16)
            part = lax.optimization_barrier(part.reshape(width, level_count, row_count))
            result.append(send(part.transpose(1, 2, 0), shift))
        return result

    coefficients = row_call(
        first_kernel,
        (state_grid, mixer, scale, forward),
        (1, None, 0, None),
        coeff_shape,
        lat_count,
        jnp.bfloat16,
        block,
    )
    bands = bands_of(clone(solve(coefficients)))
    coefficients = row_call(
        functools.partial(middle_kernel, lat_count),
        (backward, mixer, scale, forward, *bands),
        (None, None, 0, None) + (1,) * lat_count,
        coeff_shape,
        lat_count,
        jnp.bfloat16,
        block,
    )
    bands = bands_of(solve(coefficients))
    (state_grid,) = row_call(
        last_kernel,
        (backward, *bands),
        (None,) + (1,) * lat_count,
        state_grid.shape,
        1,
        jnp.float32,
        block,
    )
    return state_grid[None]


def solution(mesh):
    placed = (
        P("traj", None, "lat", None),
        P("traj"),
        P(),
        P("lat"),
        P("lat", None, None),
        P(),
        P(),
        P(),
    )
    return jax.shard_map(
        local, mesh=mesh, in_specs=placed, out_specs=P("traj", None, "lat", None), check_vma=False
    )
```

```python
import functools
import math

import jax
import jax.numpy as jnp
from jax import lax
from jax.experimental import pallas as pl
from jax.experimental.pallas import tpu as pltpu
from jax.sharding import PartitionSpec as P

time_step = 0.3
cubic_rate = 0.1


def clone_sources(counts):
    living = (counts > 0).astype(jnp.int32)
    surplus_end = jnp.cumsum(jnp.maximum(counts - 1, 0), dtype=jnp.int32)
    killed_rank = jnp.cumsum(1 - living, dtype=jnp.int32) - (1 - living)
    pulled = jnp.sum(
        (surplus_end[None, :] <= killed_rank[:, None]).astype(jnp.int32), axis=1, dtype=jnp.int32
    )
    members = jnp.arange(counts.shape[0], dtype=jnp.int32)
    return jnp.where(living > 0, members, pulled)


def fourier_tables(wavenumber, component, longitudes):
    positions = jnp.arange(longitudes, dtype=jnp.int32)
    product_index = positions[:, None] * wavenumber[None, :] % longitudes
    angles = 2.0 * math.pi / longitudes * product_index.astype(jnp.float32)
    signed = jnp.where(component[None, :] == 0, jnp.cos(angles), -jnp.sin(angles))
    factor = jnp.where(wavenumber == 0, 1.0, 2.0).astype(jnp.float32)
    return (signed.astype(jnp.bfloat16), (factor[None, :] * signed).T.astype(jnp.bfloat16))


def mode_divisor(mode_rates, degree_count):
    degrees = jnp.arange(degree_count, dtype=jnp.float32)
    degree_ratio = degrees * (degrees + 1.0) / (degree_count * (degree_count + 1.0))
    return 1.0 + mode_rates[:, None] * degree_ratio[None, :]


def grid_section(state_grid, mixing, lat_scale, forward):
    level_count, row_count, col_count = state_grid.shape
    rounded = state_grid.astype(jnp.bfloat16)
    mixing_term = jnp.dot(
        mixing,
        rounded.reshape(level_count, row_count * col_count),
        preferred_element_type=jnp.float32,
    ).reshape(level_count, row_count, col_count)
    tendency = state_grid + time_step * (
        mixing_term - cubic_rate * state_grid * state_grid * state_grid
    )
    grid_rounded = tendency.astype(jnp.bfloat16).reshape(level_count * row_count, col_count)
    fourier_sums = jnp.dot(grid_rounded, forward, preferred_element_type=jnp.float32)
    fourier_sums = fourier_sums.reshape(level_count, row_count, forward.shape[1])
    return (fourier_sums * lat_scale[None, :, None]).astype(jnp.bfloat16)


def implicit_solve(spectral, to_modes, from_modes, divisor):
    modal = (
        jnp.einsum("kl,pmln->pmkn", to_modes, spectral, precision=lax.Precision.HIGHEST)
        / divisor[None, None]
    )
    return jnp.einsum("lk,pmkn->pmln", from_modes, modal, precision=lax.Precision.HIGHEST).astype(
        jnp.bfloat16
    )


def spread_mixing(mixing):
    level_count = mixing.shape[0]
    at = jnp.arange(8 * level_count, dtype=jnp.int32)
    picks = (at[:, None] // 8 == jnp.arange(level_count)[None, :]).astype(mixing.dtype)
    tall = jnp.dot(picks, mixing, preferred_element_type=jnp.float32).astype(mixing.dtype)
    both = jnp.dot(tall, picks.T, preferred_element_type=jnp.float32)
    same_row = at[:, None] % 8 == at[None, :] % 8
    return jnp.where(same_row, both, 0.0).astype(mixing.dtype)


def to_coefficients(values, mixer, scale, forward):
    level_count, rows, longitudes = values.shape
    flat = values.reshape(level_count * rows, longitudes)
    mixed = jnp.dot(mixer, flat.astype(jnp.bfloat16), preferred_element_type=jnp.float32)
    tendency = flat + time_step * (mixed - cubic_rate * flat * flat * flat)
    sums = jnp.dot(tendency.astype(jnp.bfloat16), forward, preferred_element_type=jnp.float32)
    return sums.reshape(level_count, rows, forward.shape[1]) * scale[None, :, :1]


def from_bands(bands, backward):
    level_count, rows, width = bands[0].shape
    total = None
    for part, band in enumerate(bands):
        term = jnp.dot(
            band[...].reshape(level_count * rows, width),
            backward[part * width : (part + 1) * width, :],
            preferred_element_type=jnp.float32,
        )
        total = term if total is None else total + term
    return total.reshape(level_count, rows, backward.shape[1])


def split_columns(pieces, out_refs):
    whole = jnp.concatenate(pieces, axis=1)
    width = out_refs[0].shape[2]
    for part, out_ref in enumerate(out_refs):
        out_ref[...] = whole[:, :, part * width : (part + 1) * width].astype(jnp.bfloat16)


def first_kernel(grid_ref, mixer_ref, scale_ref, forward_ref, *out_refs):
    pieces = []
    for low in range(0, grid_ref.shape[1], 8):
        values = grid_ref[:, low : low + 8, :]
        scale = scale_ref[low : low + 8, :]
        pieces.append(to_coefficients(values, mixer_ref[...], scale, forward_ref[...]))
    split_columns(pieces, out_refs)


def middle_kernel(parts, backward_ref, mixer_ref, scale_ref, forward_ref, *refs):
    out_refs = refs[parts:]
    whole = from_bands(refs[:parts], backward_ref[...])
    pieces = []
    for low in range(0, whole.shape[1], 8):
        scale = scale_ref[low : low + 8, :]
        values = whole[:, low : low + 8, :]
        pieces.append(to_coefficients(values, mixer_ref[...], scale, forward_ref[...]))
    split_columns(pieces, out_refs)


def last_kernel(backward_ref, *refs):
    refs[-1][...] = from_bands(refs[:-1], backward_ref[...])


def bands_kernel(rows_ref, table_ref, out_ref):
    for at in range(rows_ref.shape[0]):
        out_ref[at] = lax.dot_general(
            rows_ref[at],
            table_ref[at],
            (((1,), (1,)), ((), ())),
            preferred_element_type=jnp.float32,
        ).astype(jnp.bfloat16)


def wave_bands(rows, table):
    shape = (rows.shape[0], rows.shape[1], table.shape[1])
    return pl.pallas_call(
        bands_kernel,
        grid=(shape[0] // 16,),
        in_specs=[by_rows(rows.shape, 0, 16), by_rows(table.shape, 0, 16)],
        out_specs=by_rows(shape, 0, 16),
        out_shape=jax.ShapeDtypeStruct(shape, jnp.bfloat16),
        cost_estimate=pl.CostEstimate(
            flops=2 * math.prod(shape) * rows.shape[2],
            bytes_accessed=2 * (rows.size + table.size + math.prod(shape)),
            transcendentals=0,
        ),
        compiler_params=pltpu.CompilerParams(vmem_limit_bytes=32 * 1024 * 1024),
    )(rows, table)


def fixed(array):
    return pl.BlockSpec(array.shape, lambda step: (0,) * array.ndim)


def by_rows(shape, axis, block):
    sizes = tuple(block if at == axis else size for at, size in enumerate(shape))
    return pl.BlockSpec(sizes, lambda step: tuple(step if at == axis else 0 for at in range(len(shape))))


def row_call(kernel, operands, row_axes, out_shape, out_count, out_type, block):
    rows = out_shape[1]
    specs = [
        fixed(op) if axis is None else by_rows(op.shape, axis, block)
        for op, axis in zip(operands, row_axes)
    ]
    return pl.pallas_call(
        kernel,
        grid=(rows // block,),
        in_specs=specs,
        out_specs=[by_rows(out_shape, 1, block)] * out_count,
        out_shape=[jax.ShapeDtypeStruct(out_shape, out_type)] * out_count,
        compiler_params=pltpu.CompilerParams(vmem_limit_bytes=40 * 1024 * 1024),
    )(*operands)


def local(ensemble, counts, mixing, weights, legendre, to_modes, from_modes, mode_rates):
    traj_count = lax.axis_size("traj")
    lat_count = lax.axis_size("lat")
    local_waves = legendre.shape[0]
    degree_count = legendre.shape[2]
    total_waves = local_waves * lat_count
    longitudes = ensemble.shape[3]
    columns = jnp.arange(2 * total_waves, dtype=jnp.int32)
    within = columns % (2 * local_waves)
    width = 2 * local_waves
    block = 16
    whole_blocks = width % 128 == 0 and ensemble.shape[2] % block == 0
    if whole_blocks:
        wave_of, component = within // 2, within % 2
    else:
        wave_of, component = within % local_waves, within // local_waves
    wavenumber = columns // width * local_waves + wave_of
    forward, backward = fourier_tables(wavenumber, component, longitudes)
    lat_scale = weights / longitudes
    divisor = mode_divisor(mode_rates, degree_count)
    sources = clone_sources(lax.all_gather(counts, "traj", axis=0, tiled=True))

    def to_spectral(received):
        split_parts = received.reshape(received.shape[0], received.shape[1], 2, local_waves)
        return jnp.einsum(
            "ljpm,mjn->pmln", split_parts, legendre, preferred_element_type=jnp.float32
        )

    def to_grid(received):
        flat_rows = received.reshape(received.shape[0] * received.shape[1], received.shape[2])
        result_grid = jnp.dot(flat_rows, backward, preferred_element_type=jnp.float32)
        return result_grid.reshape(received.shape[0], received.shape[1], longitudes)

    def to_implicit(coefficients):
        spectral = to_spectral(
            lax.all_to_all(coefficients, "lat", split_axis=2, concat_axis=1, tiled=True)
        )
        return implicit_solve(spectral, to_modes, from_modes, divisor)

    def clone(implicit):
        pieces = implicit.reshape(traj_count, -1, degree_count)
        spread = lax.all_to_all(pieces, "traj", split_axis=0, concat_axis=0, tiled=True)
        chosen = jnp.take(spread, sources, axis=0)
        merged = lax.all_to_all(chosen, "traj", split_axis=0, concat_axis=0, tiled=True)
        return merged.reshape(implicit.shape)

    def to_band_grid(implicit):
        band_parts = jnp.einsum(
            "mjn,pmln->ljpm", legendre, implicit, preferred_element_type=jnp.float32
        )
        band_parts = band_parts.astype(jnp.bfloat16)
        band_parts = band_parts.reshape(band_parts.shape[0], band_parts.shape[1], 2 * local_waves)
        return to_grid(lax.all_to_all(band_parts, "lat", split_axis=1, concat_axis=2, tiled=True))

    state_grid = ensemble[0]
    level_count, row_count, col_count = state_grid.shape
    if not whole_blocks:
        implicit = clone(to_implicit(grid_section(state_grid, mixing, lat_scale, forward)))
        state_grid = to_band_grid(implicit)
        state_grid = to_band_grid(
            to_implicit(grid_section(state_grid, mixing, lat_scale, forward))
        )
        return state_grid[None]

    mixer = spread_mixing(mixing)
    scale = jnp.broadcast_to(lat_scale[:, None], (row_count, 128))
    coeff_shape = (level_count, row_count, width)
    me = lax.axis_index("lat")
    shifts = range(lat_count)
    tables = legendre.reshape(local_waves, lat_count, row_count, degree_count)

    def take(array, part, axis):
        return lax.dynamic_index_in_dim(array, part % lat_count, axis, keepdims=False)

    send_tables = [take(tables, me + shift, 1) for shift in shifts]
    recv_tables = [take(tables, me - shift + lat_count, 1) for shift in shifts]
    forward_parts = forward.reshape(longitudes, lat_count, width)
    forward = jnp.concatenate([take(forward_parts, me + shift, 1) for shift in shifts], axis=1)
    backward_parts = backward.reshape(lat_count, width, longitudes)
    backward = jnp.concatenate(
        [take(backward_parts, me - shift + lat_count, 0) for shift in shifts], axis=0
    )

    def send(array, shift):
        if shift == 0:
            return array
        pairs = [(at, (at + shift) % lat_count) for at in range(lat_count)]
        return lax.ppermute(array, "lat", pairs)

    def solve(blocks):
        spectral = 0.0
        for shift in shifts:
            arrived = send(blocks[shift], shift)
            rows = lax.optimization_barrier(arrived.transpose(2, 0, 1))
            rows = rows.reshape(local_waves, 2 * level_count, row_count)
            spectral += jnp.einsum(
                "mrj,mjn->mrn", rows, recv_tables[shift], preferred_element_type=jnp.float32
            )
        spectral = spectral.reshape(1, width, level_count, degree_count)
        return implicit_solve(spectral, to_modes, from_modes, divisor)

    def bands_of(implicit):
        rows = implicit.reshape(local_waves, 2 * level_count, degree_count)
        result = []
        for shift in shifts:
            part = wave_bands(rows, send_tables[shift])
            part = lax.optimization_barrier(part.reshape(width, level_count, row_count))
            result.append(send(part.transpose(1, 2, 0), shift))
        return result

    coefficients = row_call(
        first_kernel,
        (state_grid, mixer, scale, forward),
        (1, None, 0, None),
        coeff_shape,
        lat_count,
        jnp.bfloat16,
        block,
    )
    bands = bands_of(clone(solve(coefficients)))
    coefficients = row_call(
        functools.partial(middle_kernel, lat_count),
        (backward, mixer, scale, forward, *bands),
        (None, None, 0, None) + (1,) * lat_count,
        coeff_shape,
        lat_count,
        jnp.bfloat16,
        block,
    )
    bands = bands_of(solve(coefficients))
    (state_grid,) = row_call(
        last_kernel,
        (backward, *bands),
        (None,) + (1,) * lat_count,
        state_grid.shape,
        1,
        jnp.float32,
        block,
    )
    return state_grid[None]


def solution(mesh):
    placed = (
        P("traj", None, "lat", None),
        P("traj"),
        P(),
        P("lat"),
        P("lat", None, None),
        P(),
        P(),
        P(),
    )
    return jax.shard_map(
        local, mesh=mesh, in_specs=placed, out_specs=P("traj", None, "lat", None), check_vma=False
    )
```
